32 devices in a mesh: blocks: 2 (over x), slab: 16 (over z, y, core).
Axes of the slice: x: 2, y: 2, z: 4, core: 2. Of those that a mesh axis runs over, the one named last changes fastest.
Arguments:
- estimate: float32 [64, 256, 128], P('blocks', 'slab'), parts along dimension 0, may hold values from 0.25 to 8, as said below
- raw_views: float32 [6, 64, 256, 128], P(None, 'blocks', 'slab'), parts along dimension 1, may hold values from 0.1 to 30, as said below
- psf_taps: float32 [6, 3, 31], replicated, may hold values from 0 to 1, as said below
Outputs:
- restored: float32 [64, 256, 128], P('blocks', 'slab'), parts along dimension 0
The draws below stay inside these ranges and needn't reach their ends.
There are 2 independent parts, one for each index of `blocks`. The reference program is written for one: setup_inputs(seed, part) draws one part's arguments, and reference() takes and returns one part's arrays. A program takes and returns all parts, laid end to end along the dimension named above; an argument that names none is the same for every part. Nothing has to cross between parts.
Inputs may be any that keep to these rules, and one draw needn't show every extreme that they name: `estimate`: positive. `raw_views`: positive. `psf_taps`: every tap is positive, and each view's taps along each dimension sum to 1.
All inputs are finite; a program needn't handle non-finite values.
Results may differ from the reference program's by a relative error of at most 0.0001.
Values sent between devices are 32-bit elements; how exact they have to be, the bound alone decides.
A program may use at most 64 MiB of HBM per device.

```python
import math
import jax
import jax.numpy as jnp
from jax import lax

VIEWS = 6
TAPS = 31
ITERS = 2
DEPTH = 32
X = 128
Y = 256


def ramp_rows():
    row_index = jnp.arange(Y, dtype=jnp.float32)
    return (1.0 + 2.0 * row_index / (Y - 1)).reshape(1, Y, 1)


def falling_rows():
    row_index = jnp.arange(Y, dtype=jnp.float32)
    return (3.0 - 2.0 * row_index / (Y - 1)).reshape(1, Y, 1)


def draw_estimate(key, part):
    key_base = jax.random.fold_in(key, 11)
    shape_full = (DEPTH, Y, X)
    base_values = jnp.exp(jax.random.uniform(key_base, shape_full, jnp.float32, math.log(0.5), math.log(2.0)))
    return base_values * ramp_rows()


def draw_raw_views(key, part):
    key_base = jax.random.fold_in(key, 23)
    key_factor = jax.random.fold_in(key, 29)
    shape_full = (VIEWS, DEPTH, Y, X)
    factor = jnp.exp(jax.random.uniform(key_factor, (VIEWS, 1, 1, 1), jnp.float32, math.log(0.5), math.log(2.0)))
    base_values = jnp.exp(jax.random.uniform(key_base, shape_full, jnp.float32, math.log(0.2), math.log(5.0)))
    return base_values * factor * falling_rows()[None]


def draw_psf_taps(key, part):
    key_sigma = jax.random.fold_in(key, 37)
    key_rough = jax.random.fold_in(key, 41)
    lows = jnp.array([3.0, 2.0, 1.5], jnp.float32).reshape(1, 3, 1)
    highs = jnp.array([8.0, 6.0, 4.0], jnp.float32).reshape(1, 3, 1)
    unit = jax.random.uniform(key_sigma, (VIEWS, 3, 1), jnp.float32)
    sigma = jnp.exp(jnp.log(lows) + unit * (jnp.log(highs) - jnp.log(lows)))
    offsets = (jnp.arange(TAPS, dtype=jnp.float32) - (TAPS - 1) / 2.0).reshape(1, 1, TAPS)
    bumps = jnp.exp(-offsets * offsets / (2.0 * sigma * sigma)) + 0.02
    rough = jax.random.uniform(key_rough, (VIEWS, 3, TAPS), jnp.float32, 0.6, 1.4)
    shaped = bumps * rough
    return shaped / jnp.sum(shaped, axis=2, keepdims=True)


def setup_inputs(seed: int = 0, part: int = 0) -> dict:
    splits = jax.random.split(jax.random.key(seed), 4)
    own_keys = jax.random.split(jax.random.fold_in(splits[3], part), 4)
    estimate = draw_estimate(jax.random.fold_in(jax.random.fold_in(splits[3], part), 71), part)
    raw_views = draw_raw_views(jax.random.fold_in(jax.random.fold_in(splits[3], part), 71), part)
    psf_taps = draw_psf_taps(jax.random.fold_in(splits[3], 71), part)
    return dict(estimate=estimate, raw_views=raw_views, psf_taps=psf_taps)


def along_dim(volume, coeffs, dim_index):
    extent = volume.shape[dim_index]
    margin = coeffs.shape[0] // 2
    widths = [(0, 0)] * volume.ndim
    widths[dim_index] = (margin, margin)
    padded = jnp.pad(volume, widths)
    running = jnp.zeros_like(volume)
    for offset in range(coeffs.shape[0]):
        running = running + coeffs[offset] * lax.slice_in_dim(padded, offset, offset + extent, axis=dim_index)
    return running


def forward(volume, kernel):
    volume = along_dim(volume, kernel[0], 0)
    volume = along_dim(volume, kernel[1], 1)
    return along_dim(volume, kernel[2], 2)


def adjoint(volume, kernel):
    return forward(volume, kernel[:, ::-1])


def reference(estimate, raw_views, psf_taps):
    view_total = jnp.sum(raw_views, axis=(1, 2, 3))
    current = estimate
    for iteration in range(ITERS):
        blurred = lax.map(lambda kernel: forward(current, kernel), psf_taps)
        scale = jnp.sum(blurred, axis=(1, 2, 3)) / view_total
        ratio = scale.reshape(-1, 1, 1, 1) * raw_views / blurred
        logs = lax.map(lambda pair: jnp.log(adjoint(pair[0], pair[1])), (ratio, psf_taps))
        current = current * jnp.exp(jnp.mean(logs, axis=0))
    return current
```

```python
import jax
import jax.numpy as jnp
from jax import lax
from jax.experimental import pallas as pl
from jax.experimental.pallas import tpu as pltpu
from jax.sharding import PartitionSpec as P

ITERS = 2
F32 = jnp.float32
BF16 = jnp.bfloat16
MESH = pl.DeviceIdType.MESH


def split(x):
    hi = x.astype(BF16)
    return hi, (x - hi.astype(F32)).astype(BF16)


def dot(a, b):
    return jnp.dot(a, b, preferred_element_type=F32)


def iota(shape, dim):
    return lax.broadcasted_iota(jnp.int32, shape, dim)


def build_matrices(v, tap_pad, ay, ayt, wx, mz):
    near = jnp.abs(iota((128, 128), 0) - iota((128, 128), 1)) <= 15

    def band(d):
        row = jnp.broadcast_to(tap_pad[v, pl.ds(d, 1), :], (128, 128))
        return jnp.where(near, pltpu.roll(row, 113, 1, stride=1, stride_axis=0), 0.0)

    def placed(block, width):
        hi, lo = (p.astype(F32) for p in split(block))
        zero = jnp.zeros_like(hi)
        hi, lo = jnp.concatenate([hi, zero], 1), jnp.concatenate([lo, zero], 1)
        return (hi + pltpu.roll(hi, width, 1) + pltpu.roll(lo, 2 * width, 1)).astype(BF16)

    ty = band(1)
    ay[pl.ds(pl.multiple_of(v * 48, 16), 48), :] = placed(ty[16:64], 80)
    ayt[v] = placed(ty.T[16:32], 48)[:, :144]

    tx = band(2)
    for direction, w in ((0, tx.T), (1, tx)):
        hi, lo = split(w)
        wx[direction, v, 0:128, 0:128] = hi
        wx[direction, v, 128:256, 0:128] = hi
        wx[direction, v, 0:128, 128:256] = lo
        wx[direction, v, 128:256, 128:256] = jnp.zeros_like(hi)

    tz = band(0)
    spread = (iota((256, 128), 0) // 8 == iota((256, 128), 1)).astype(F32).astype(BF16)
    spread_t = (iota((128, 256), 0) == iota((128, 256), 1) // 8).astype(F32).astype(BF16)
    same = (iota((256, 256), 0) % 8) == (iota((256, 256), 1) % 8)
    for direction, m in ((0, tz), (1, tz.T)):
        for half, part in enumerate(split(m)):
            wide = dot(dot(spread, part).astype(BF16), spread_t)
            mz[direction, v, 256 * half : 256 * half + 256, :] = jnp.where(same, wide, 0.0).astype(BF16)


def columns_then_planes(pair, w, m):
    r = dot(pair, w)
    rhs = jnp.concatenate(split(r[:, :128] + r[:, 128:]), 1)
    q = dot(m, rhs)
    return (q[:256, :128] + q[:256, 128:]) + (q[256:, :128] + q[256:, 128:])


def kernel(
    n, views,
    est, raw, taps, out,
    tap_pad, ay, ayt, wx, mz, halo, raw_halo, frame, g_pair, ratio3, k_pair, acc, cur, stat, msg, msgs,
    est_send, est_recv, raw_send, raw_recv, msg_send, msg_recv,
):
    me = lax.axis_index("slab")
    has_left, has_right = me > 0, me < n - 1
    left, right = lax.rem(me + n - 1, n), lax.rem(me + 1, n)

    barrier = pltpu.get_barrier_semaphore()

    def greet(d, _):
        pl.semaphore_signal(barrier, inc=1, device_id={"slab": lax.rem(me + d, n)}, device_id_type=MESH)
        return 0

    lax.fori_loop(1, n, greet, 0)
    pl.semaphore_wait(barrier, n - 1)

    def copy(src, dst, send, recv, to):
        return pltpu.make_async_remote_copy(
            src_ref=src, dst_ref=dst, send_sem=send, recv_sem=recv, device_id={"slab": to}, device_id_type=MESH
        )

    def est_copies(it, source):
        srcs = (source, source, halo.at[it, 0], halo.at[it, 1])
        tos = (right, left, right, left)
        return [
            copy(srcs[k], halo.at[it, k], est_send.at[it, k], est_recv.at[it, k], tos[k]) for k in range(4)
        ]

    both = has_left & has_right
    sends = (has_right, has_left, both, both)
    recvs = (has_left, has_right, me > 1, me < n - 2)

    def raw_copy(v, k):
        return copy(raw.at[v], raw_halo.at[k, v], raw_send.at[v, k], raw_recv.at[v, k], (right, left)[k])

    first = est_copies(0, est)
    pl.when(has_right)(first[0].start)
    pl.when(has_left)(first[1].start)

    tap_pad[...] = jnp.zeros_like(tap_pad)
    for v in range(views):
        tap_pad[v, 0:3, 0:31] = taps[v]
    stat[...] = jnp.zeros_like(stat)
    frame[:, 240:256, :] = jnp.zeros((32, 16, 128), BF16)
    for it in range(ITERS):
        for k, there in enumerate(recvs):
            @pl.when(jnp.logical_not(there))
            def _():
                halo[it, k] = jnp.zeros((32, 16, 128), F32)

    def put_block(b, ref_block):
        hi, lo = split(ref_block[...])
        frame[:, 16 * b : 16 * b + 16, :] = hi
        frame[:, 80 + 16 * b : 96 + 16 * b, :] = lo
        frame[:, 160 + 16 * b : 176 + 16 * b, :] = hi

    def exchange(it, copies, source, meanwhile):
        put_block(2, source)
        for k in (0, 1):
            pl.when(recvs[k])(copies[k].wait_recv)
            pl.when(sends[2 + k])(copies[2 + k].start)
        meanwhile()
        put_block(1, halo.at[it, 0])
        put_block(3, halo.at[it, 1])
        for k in (2, 3):
            pl.when(recvs[k])(copies[k].wait_recv)
        put_block(0, halo.at[it, 2])
        put_block(4, halo.at[it, 3])

    def start_raw():
        def go(v, _):
            pl.when(has_right)(raw_copy(v, 0).start)
            pl.when(has_left)(raw_copy(v, 1).start)
            return 0

        lax.fori_loop(0, views, go, 0)

        def build(v, _):
            build_matrices(v, tap_pad, ay, ayt, wx, mz)
            return 0

        lax.fori_loop(0, views, build, 0)

    def rows_forward():
        def step(k, _):
            rhs = jnp.concatenate([frame[2 * k], frame[2 * k + 1]], 1)
            rows = pl.ds(pl.multiple_of(16 * k, 16), 16)
            for v in range(views):
                res = dot(ay[48 * v : 48 * v + 48, :], rhs)
                for t in range(6):
                    two = jnp.concatenate([res[8 * t : 8 * t + 8, :128], res[8 * t : 8 * t + 8, 128:]], 0)
                    hi, lo = split(two)
                    g_pair[v, t, rows, 0:128] = hi
                    g_pair[v, t, rows, 128:256] = lo
            return 0

        lax.fori_loop(0, 16, step, 0)

    def blur_and_ratio(it, v):
        w, m = wx[0, v], mz[0, v]
        blurred = [columns_then_planes(g_pair[v, t], w, m).reshape(32, 8, 128) for t in range(6)]
        total = jnp.sum(blurred[2] + blurred[3], axis=0)
        stat[2 * it, pl.ds(v, 1), :] = jnp.sum(total, axis=0, keepdims=True)
        if it == 0:
            counts = jnp.sum(raw[v, :, 0:8, :] + raw[v, :, 8:16, :], axis=0)
            stat[1, pl.ds(v, 1), :] = jnp.sum(counts, axis=0, keepdims=True)
            pl.when(has_left)(raw_copy(v, 0).wait_recv)
            pl.when(has_right)(raw_copy(v, 1).wait_recv)
        for b, (block, there) in enumerate(
            ((raw_halo.at[0, v], has_left), (raw.at[v], None), (raw_halo.at[1, v], has_right))
        ):
            value = block[...] / jnp.concatenate([blurred[2 * b], blurred[2 * b + 1]], 1)
            if there is not None:
                value = jnp.where(there, value, 0.0)
            hi, lo = split(value)
            ratio3[v, :, 16 * b : 16 * b + 16, :] = hi
            ratio3[v, :, 48 + 16 * b : 64 + 16 * b, :] = lo
            ratio3[v, :, 96 + 16 * b : 112 + 16 * b, :] = hi

    def adjoint_log(v):
        a = ayt[v]
        for k in range(16):
            res = dot(a, jnp.concatenate([ratio3[v, 2 * k], ratio3[v, 2 * k + 1]], 1))
            for t in range(2):
                two = jnp.concatenate([res[8 * t : 8 * t + 8, :128], res[8 * t : 8 * t + 8, 128:]], 0)
                hi, lo = split(two)
                k_pair[t, 16 * k : 16 * k + 16, 0:128] = hi
                k_pair[t, 16 * k : 16 * k + 16, 128:256] = lo
        w, m = wx[1, v], mz[1, v]
        for t in range(2):
            acc[t] += jnp.log(columns_then_planes(k_pair[t], w, m))

    def msg_copy(d):
        return copy(msg, msgs.at[d], msg_send.at[d], msg_recv.at[d], lax.rem(me + d, n))

    exchange(0, first, est, start_raw)
    rows_forward()
    acc[...] = jnp.zeros_like(acc)

    def view0(v, _):
        blur_and_ratio(0, v)
        adjoint_log(v)
        return 0

    lax.fori_loop(0, views, view0, 0)
    for t in range(2):
        cur[:, 8 * t : 8 * t + 8, :] = est[:, 8 * t : 8 * t + 8, :] * jnp.exp(
            acc[t] * (1.0 / views)
        ).reshape(32, 8, 128)

    second = est_copies(1, cur)
    pl.when(has_right)(second[0].start)
    pl.when(has_left)(second[1].start)
    exchange(1, second, cur, lambda: None)
    rows_forward()
    acc[...] = jnp.zeros_like(acc)

    def view1(v, _):
        blur_and_ratio(1, v)
        return 0

    lax.fori_loop(0, views, view1, 0)

    lane = iota((8, 128), 1)
    s = [jnp.sum(stat[k], axis=1, keepdims=True) for k in range(3)]
    msg[...] = jnp.where(lane == 0, s[0], jnp.where(lane == 1, s[1], s[2]))

    def send_msg(d, _):
        msg_copy(d).start()
        return 0

    lax.fori_loop(1, n, send_msg, 0)

    def view2(v, _):
        adjoint_log(v)
        return 0

    lax.fori_loop(0, views, view2, 0)

    def take_msg(d, total):
        msg_copy(d).wait()
        return total + msgs[d]

    total = lax.fori_loop(1, n, take_msg, msg[...])
    valid = (iota((8, 128), 0) < views) & (lane < 3)
    logs = jnp.log(jnp.where(valid, total, 1.0)) * jnp.where(lane == 1, -2.0, 1.0)
    log_scale = jnp.sum(jnp.sum(logs, axis=1, keepdims=True), axis=0, keepdims=True)
    for t in range(2):
        out[:, 8 * t : 8 * t + 8, :] = cur[:, 8 * t : 8 * t + 8, :] * jnp.exp(
            (acc[t] + log_scale) * (1.0 / views)
        ).reshape(32, 8, 128)

    for copies in (first, second):
        for k in range(4):
            pl.when(sends[k])(copies[k].wait_send)

    def drain(v, _):
        pl.when(has_right)(raw_copy(v, 0).wait_send)
        pl.when(has_left)(raw_copy(v, 1).wait_send)
        return 0

    lax.fori_loop(0, views, drain, 0)


def per_device(estimate, raw_views, psf_taps):
    n = lax.axis_size("slab")
    views = raw_views.shape[0]
    vmem = pl.BlockSpec(memory_space=pltpu.VMEM)
    dma = pltpu.SemaphoreType.DMA
    return pl.pallas_call(
        lambda *refs: kernel(n, views, *refs),
        out_shape=jax.ShapeDtypeStruct(estimate.shape, F32),
        in_specs=[vmem] * 3,
        out_specs=vmem,
        scratch_shapes=[
            pltpu.VMEM((views, 8, 128), F32),
            pltpu.VMEM((views * 48, 256), BF16),
            pltpu.VMEM((views, 16, 144), BF16),
            pltpu.VMEM((2, views, 256, 256), BF16),
            pltpu.VMEM((2, views, 512, 256), BF16),
            pltpu.VMEM((ITERS, 4, 32, 16, 128), F32),
            pltpu.VMEM((2, views, 32, 16, 128), F32),
            pltpu.VMEM((32, 256, 128), BF16),
            pltpu.VMEM((views, 6, 256, 256), BF16),
            pltpu.VMEM((views, 32, 144, 128), BF16),
            pltpu.VMEM((2, 256, 256), BF16),
            pltpu.VMEM((2, 256, 128), F32),
            pltpu.VMEM((32, 16, 128), F32),
            pltpu.VMEM((3, 8, 128), F32),
            pltpu.VMEM((8, 128), F32),
            pltpu.VMEM((n, 8, 128), F32),
            dma((ITERS, 4)), dma((ITERS, 4)), dma((views, 2)), dma((views, 2)), dma((n,)), dma((n,)),
        ],
        compiler_params=pltpu.CompilerParams(
            collective_id=0, has_side_effects=True, vmem_limit_bytes=56 * 1024 * 1024
        ),
    )(estimate, raw_views, psf_taps)


def solution(mesh):
    placed = (P("blocks", "slab", None), P(None, "blocks", "slab", None), P())
    return jax.shard_map(
        per_device, mesh=mesh, in_specs=placed, out_specs=P("blocks", "slab", None), check_vma=False
    )
```

```python
import jax
import jax.numpy as jnp
from jax import lax
from jax.experimental import pallas as pl
from jax.experimental.pallas import tpu as pltpu
from jax.sharding import PartitionSpec as P

ITERS = 2
F32 = jnp.float32
BF16 = jnp.bfloat16
MESH = pl.DeviceIdType.MESH


def split(x):
    hi = x.astype(BF16)
    return hi, (x - hi.astype(F32)).astype(BF16)


def dot(a, b):
    return jnp.dot(a, b, preferred_element_type=F32)


def iota(shape, dim):
    return lax.broadcasted_iota(jnp.int32, shape, dim)


def build_matrices(v, tap_pad, ay, ayt, wx, mz):
    near = jnp.abs(iota((128, 128), 0) - iota((128, 128), 1)) <= 15

    def band(d):
        row = jnp.broadcast_to(tap_pad[v, pl.ds(d, 1), :], (128, 128))
        return jnp.where(near, pltpu.roll(row, 113, 1, stride=1, stride_axis=0), 0.0)

    def placed(block, width):
        hi, lo = (p.astype(F32) for p in split(block))
        zero = jnp.zeros_like(hi)
        hi, lo = jnp.concatenate([hi, zero], 1), jnp.concatenate([lo, zero], 1)
        return (hi + pltpu.roll(hi, width, 1) + pltpu.roll(lo, 2 * width, 1)).astype(BF16)

    ty = band(1)
    ay[pl.ds(pl.multiple_of(v * 48, 16), 48), :] = placed(ty[16:64], 80)
    ayt[v] = placed(ty.T[16:32], 48)[:, :144]

    tx = band(2)
    for direction, w in ((0, tx.T), (1, tx)):
        hi, lo = split(w)
        wx[direction, v, 0:128, 0:128] = hi
        wx[direction, v, 128:256, 0:128] = hi
        wx[direction, v, 0:128, 128:256] = lo
        wx[direction, v, 128:256, 128:256] = jnp.zeros_like(hi)

    tz = band(0)
    spread = (iota((256, 128), 0) // 8 == iota((256, 128), 1)).astype(F32).astype(BF16)
    spread_t = (iota((128, 256), 0) == iota((128, 256), 1) // 8).astype(F32).astype(BF16)
    same = (iota((256, 256), 0) % 8) == (iota((256, 256), 1) % 8)
    for direction, m in ((0, tz), (1, tz.T)):
        for half, part in enumerate(split(m)):
            wide = dot(dot(spread, part).astype(BF16), spread_t)
            mz[direction, v, 256 * half : 256 * half + 256, :] = jnp.where(same, wide, 0.0).astype(BF16)


def columns_then_planes(pair, w, m):
    r = dot(pair, w)
    rhs = jnp.concatenate(split(r[:, :128] + r[:, 128:]), 1)
    q = dot(m, rhs)
    return (q[:256, :128] + q[:256, 128:]) + (q[256:, :128] + q[256:, 128:])


def kernel(
    n, views,
    est, raw, taps, out,
    tap_pad, ay, ayt, wx, mz, halo, raw_halo, frame, g_pair, ratio3, k_pair, acc, cur, stat, msg, msgs,
    est_send, est_recv, raw_send, raw_recv, msg_send, msg_recv,
):
    me = lax.axis_index("slab")
    has_left, has_right = me > 0, me < n - 1
    left, right = lax.rem(me + n - 1, n), lax.rem(me + 1, n)

    barrier = pltpu.get_barrier_semaphore()

    def greet(d, _):
        pl.semaphore_signal(barrier, inc=1, device_id={"slab": lax.rem(me + d, n)}, device_id_type=MESH)
        return 0

    lax.fori_loop(1, n, greet, 0)
    pl.semaphore_wait(barrier, n - 1)

    def copy(src, dst, send, recv, to):
        return pltpu.make_async_remote_copy(
            src_ref=src, dst_ref=dst, send_sem=send, recv_sem=recv, device_id={"slab": to}, device_id_type=MESH
        )

    def est_copies(it, source):
        srcs = (source, source, halo.at[it, 0], halo.at[it, 1])
        tos = (right, left, right, left)
        return [
            copy(srcs[k], halo.at[it, k], est_send.at[it, k], est_recv.at[it, k], tos[k]) for k in range(4)
        ]

    both = has_left & has_right
    sends = (has_right, has_left, both, both)
    recvs = (has_left, has_right, me > 1, me < n - 2)

    def raw_copy(v, k):
        return copy(raw.at[v], raw_halo.at[k, v], raw_send.at[v, k], raw_recv.at[v, k], (right, left)[k])

    first = est_copies(0, est)
    pl.when(has_right)(first[0].start)
    pl.when(has_left)(first[1].start)

    tap_pad[...] = jnp.zeros_like(tap_pad)
    for v in range(views):
        tap_pad[v, 0:3, 0:31] = taps[v]
    stat[...] = jnp.zeros_like(stat)
    frame[:, 240:256, :] = jnp.zeros((32, 16, 128), BF16)
    for it in range(ITERS):
        for k, there in enumerate(recvs):
            @pl.when(jnp.logical_not(there))
            def _():
                halo[it, k] = jnp.zeros((32, 16, 128), F32)

    def put_block(b, ref_block):
        hi, lo = split(ref_block[...])
        frame[:, 16 * b : 16 * b + 16, :] = hi
        frame[:, 80 + 16 * b : 96 + 16 * b, :] = lo
        frame[:, 160 + 16 * b : 176 + 16 * b, :] = hi

    odd = lax.rem(me, 2) == 1

    def pass_on(copies, k):
        pl.when(recvs[k])(copies[k].wait_recv)
        pl.when(sends[2 + k])(copies[2 + k].start)

    def exchange(it, copies, source, early, meanwhile):
        pl.when(odd)(lambda: pass_on(copies, 0))
        pl.when(jnp.logical_not(odd))(lambda: pass_on(copies, 1))
        early()
        put_block(2, source)
        pl.when(odd)(lambda: pass_on(copies, 1))
        pl.when(jnp.logical_not(odd))(lambda: pass_on(copies, 0))
        meanwhile()
        put_block(1, halo.at[it, 0])
        put_block(3, halo.at[it, 1])
        for k in (2, 3):
            pl.when(recvs[k])(copies[k].wait_recv)
        put_block(0, halo.at[it, 2])
        put_block(4, halo.at[it, 3])

    def start_raw():
        def go(v, _):
            pl.when(has_right)(raw_copy(v, 0).start)
            pl.when(has_left)(raw_copy(v, 1).start)
            return 0

        lax.fori_loop(0, views, go, 0)

    def build_all():
        def build(v, _):
            build_matrices(v, tap_pad, ay, ayt, wx, mz)
            return 0

        lax.fori_loop(0, views, build, 0)

    def rows_forward():
        def step(k, _):
            rhs = jnp.concatenate([frame[2 * k], frame[2 * k + 1]], 1)
            rows = pl.ds(pl.multiple_of(16 * k, 16), 16)
            for v in range(views):
                res = dot(ay[48 * v : 48 * v + 48, :], rhs)
                for t in range(6):
                    two = jnp.concatenate([res[8 * t : 8 * t + 8, :128], res[8 * t : 8 * t + 8, 128:]], 0)
                    hi, lo = split(two)
                    g_pair[v, t, rows, 0:128] = hi
                    g_pair[v, t, rows, 128:256] = lo
            return 0

        lax.fori_loop(0, 16, step, 0)

    def blur_and_ratio(it, v):
        w, m = wx[0, v], mz[0, v]
        blurred = [columns_then_planes(g_pair[v, t], w, m).reshape(32, 8, 128) for t in range(6)]
        total = jnp.sum(blurred[2] + blurred[3], axis=0)
        stat[2 * it, pl.ds(v, 1), :] = jnp.sum(total, axis=0, keepdims=True)
        if it == 0:
            counts = jnp.sum(raw[v, :, 0:8, :] + raw[v, :, 8:16, :], axis=0)
            stat[1, pl.ds(v, 1), :] = jnp.sum(counts, axis=0, keepdims=True)
            pl.when(has_left)(raw_copy(v, 0).wait_recv)
            pl.when(has_right)(raw_copy(v, 1).wait_recv)
        for b, (block, there) in enumerate(
            ((raw_halo.at[0, v], has_left), (raw.at[v], None), (raw_halo.at[1, v], has_right))
        ):
            value = block[...] / jnp.concatenate([blurred[2 * b], blurred[2 * b + 1]], 1)
            if there is not None:
                value = jnp.where(there, value, 0.0)
            hi, lo = split(value)
            ratio3[v, :, 16 * b : 16 * b + 16, :] = hi
            ratio3[v, :, 48 + 16 * b : 64 + 16 * b, :] = lo
            ratio3[v, :, 96 + 16 * b : 112 + 16 * b, :] = hi

    def adjoint_log(v):
        a = ayt[v]
        for k in range(16):
            res = dot(a, jnp.concatenate([ratio3[v, 2 * k], ratio3[v, 2 * k + 1]], 1))
            for t in range(2):
                two = jnp.concatenate([res[8 * t : 8 * t + 8, :128], res[8 * t : 8 * t + 8, 128:]], 0)
                hi, lo = split(two)
                k_pair[t, 16 * k : 16 * k + 16, 0:128] = hi
                k_pair[t, 16 * k : 16 * k + 16, 128:256] = lo
        w, m = wx[1, v], mz[1, v]
        for t in range(2):
            acc[t] += jnp.log(columns_then_planes(k_pair[t], w, m))

    def msg_copy(d):
        return copy(msg, msgs.at[d], msg_send.at[d], msg_recv.at[d], lax.rem(me + d, n))

    exchange(0, first, est, start_raw, build_all)
    rows_forward()
    acc[...] = jnp.zeros_like(acc)

    def view0(v, _):
        blur_and_ratio(0, v)
        adjoint_log(v)
        return 0

    lax.fori_loop(0, views, view0, 0)
    for t in range(2):
        cur[:, 8 * t : 8 * t + 8, :] = est[:, 8 * t : 8 * t + 8, :] * jnp.exp(
            acc[t] * (1.0 / views)
        ).reshape(32, 8, 128)

    second = est_copies(1, cur)
    pl.when(has_right)(second[0].start)
    pl.when(has_left)(second[1].start)
    exchange(1, second, cur, lambda: None, lambda: None)
    rows_forward()
    acc[...] = jnp.zeros_like(acc)

    def view1(v, _):
        blur_and_ratio(1, v)
        return 0

    lax.fori_loop(0, views, view1, 0)

    lane = iota((8, 128), 1)
    s = [jnp.sum(stat[k], axis=1, keepdims=True) for k in range(3)]
    msg[...] = jnp.where(lane == 0, s[0], jnp.where(lane == 1, s[1], s[2]))

    def send_msg(d, _):
        msg_copy(d).start()
        return 0

    lax.fori_loop(1, n, send_msg, 0)

    def view2(v, _):
        adjoint_log(v)
        return 0

    lax.fori_loop(0, views, view2, 0)

    def take_msg(d, total):
        msg_copy(d).wait()
        return total + msgs[d]

    total = lax.fori_loop(1, n, take_msg, msg[...])
    valid = (iota((8, 128), 0) < views) & (lane < 3)
    logs = jnp.log(jnp.where(valid, total, 1.0)) * jnp.where(lane == 1, -2.0, 1.0)
    log_scale = jnp.sum(jnp.sum(logs, axis=1, keepdims=True), axis=0, keepdims=True)
    for t in range(2):
        out[:, 8 * t : 8 * t + 8, :] = cur[:, 8 * t : 8 * t + 8, :] * jnp.exp(
            (acc[t] + log_scale) * (1.0 / views)
        ).reshape(32, 8, 128)

    for copies in (first, second):
        for k in range(4):
            pl.when(sends[k])(copies[k].wait_send)

    def drain(v, _):
        pl.when(has_right)(raw_copy(v, 0).wait_send)
        pl.when(has_left)(raw_copy(v, 1).wait_send)
        return 0

    lax.fori_loop(0, views, drain, 0)


def per_device(estimate, raw_views, psf_taps):
    n = lax.axis_size("slab")
    views = raw_views.shape[0]
    vmem = pl.BlockSpec(memory_space=pltpu.VMEM)
    dma = pltpu.SemaphoreType.DMA
    return pl.pallas_call(
        lambda *refs: kernel(n, views, *refs),
        out_shape=jax.ShapeDtypeStruct(estimate.shape, F32),
        in_specs=[vmem] * 3,
        out_specs=vmem,
        scratch_shapes=[
            pltpu.VMEM((views, 8, 128), F32),
            pltpu.VMEM((views * 48, 256), BF16),
            pltpu.VMEM((views, 16, 144), BF16),
            pltpu.VMEM((2, views, 256, 256), BF16),
            pltpu.VMEM((2, views, 512, 256), BF16),
            pltpu.VMEM((ITERS, 4, 32, 16, 128), F32),
            pltpu.VMEM((2, views, 32, 16, 128), F32),
            pltpu.VMEM((32, 256, 128), BF16),
            pltpu.VMEM((views, 6, 256, 256), BF16),
            pltpu.VMEM((views, 32, 144, 128), BF16),
            pltpu.VMEM((2, 256, 256), BF16),
            pltpu.VMEM((2, 256, 128), F32),
            pltpu.VMEM((32, 16, 128), F32),
            pltpu.VMEM((3, 8, 128), F32),
            pltpu.VMEM((8, 128), F32),
            pltpu.VMEM((n, 8, 128), F32),
            dma((ITERS, 4)), dma((ITERS, 4)), dma((views, 2)), dma((views, 2)), dma((n,)), dma((n,)),
        ],
        compiler_params=pltpu.CompilerParams(
            collective_id=0, has_side_effects=True, vmem_limit_bytes=56 * 1024 * 1024
        ),
    )(estimate, raw_views, psf_taps)


def solution(mesh):
    placed = (P("blocks", "slab", None), P(None, "blocks", "slab", None), P())
    return jax.shard_map(
        per_device, mesh=mesh, in_specs=placed, out_specs=P("blocks", "slab", None), check_vma=False
    )
```

```python
import jax
import jax.numpy as jnp
from jax import lax
from jax.experimental import pallas as pl
from jax.experimental.pallas import tpu as pltpu
from jax.sharding import PartitionSpec as P

ITERS = 2
F32 = jnp.float32
BF16 = jnp.bfloat16
MESH = pl.DeviceIdType.MESH


def split(x):
    hi = x.astype(BF16)
    return hi, (x - hi.astype(F32)).astype(BF16)


def dot(a, b):
    return jnp.dot(a, b, preferred_element_type=F32)


def iota(shape, dim):
    return lax.broadcasted_iota(jnp.int32, shape, dim)


def build_matrices(v, tap_pad, ay, ayt, wx, mz):
    near = jnp.abs(iota((128, 128), 0) - iota((128, 128), 1)) <= 15

    def band(d):
        row = jnp.broadcast_to(tap_pad[v, pl.ds(d, 1), :], (128, 128))
        return jnp.where(near, pltpu.roll(row, 113, 1, stride=1, stride_axis=0), 0.0)

    def placed(block, width):
        hi, lo = (p.astype(F32) for p in split(block))
        zero = jnp.zeros_like(hi)
        hi, lo = jnp.concatenate([hi, zero], 1), jnp.concatenate([lo, zero], 1)
        return (hi + pltpu.roll(hi, width, 1) + pltpu.roll(lo, 2 * width, 1)).astype(BF16)

    ty = band(1)
    ay[pl.ds(pl.multiple_of(v * 48, 16), 48), :] = placed(ty[16:64], 80)
    ayt[v] = placed(ty.T[16:32], 48)[:, :144]

    tx = band(2)
    for direction, w in ((0, tx.T), (1, tx)):
        hi, lo = split(w)
        wx[direction, v, 0:128, 0:128] = hi
        wx[direction, v, 128:256, 0:128] = hi
        wx[direction, v, 0:128, 128:256] = lo
        wx[direction, v, 128:256, 128:256] = jnp.zeros_like(hi)

    tz = band(0)
    spread = (iota((256, 128), 0) // 8 == iota((256, 128), 1)).astype(F32).astype(BF16)
    spread_t = (iota((128, 256), 0) == iota((128, 256), 1) // 8).astype(F32).astype(BF16)
    same = (iota((256, 256), 0) % 8) == (iota((256, 256), 1) % 8)
    for direction, m in ((0, tz), (1, tz.T)):
        for half, part in enumerate(split(m)):
            wide = dot(dot(spread, part).astype(BF16), spread_t)
            mz[direction, v, 256 * half : 256 * half + 256, :] = jnp.where(same, wide, 0.0).astype(BF16)


def columns_then_planes(pair, w, m):
    r = dot(pair, w)
    rhs = jnp.concatenate(split(r[:, :128] + r[:, 128:]), 1)
    q = dot(m, rhs)
    return (q[:256, :128] + q[:256, 128:]) + (q[256:, :128] + q[256:, 128:])


def kernel(
    n, views,
    est, raw, taps, out,
    tap_pad, ay, ayt, wx, mz, halo, raw_halo, frame, g_pair, ratio3, k_pair, acc, cur, stat, msg, msgs,
    est_send, est_recv, raw_send, raw_recv, msg_send, msg_recv,
):
    me = lax.axis_index("slab")
    has_left, has_right = me > 0, me < n - 1
    left, right = lax.rem(me + n - 1, n), lax.rem(me + 1, n)

    barrier = pltpu.get_barrier_semaphore()

    def greet(d, _):
        pl.semaphore_signal(barrier, inc=1, device_id={"slab": lax.rem(me + d, n)}, device_id_type=MESH)
        return 0

    lax.fori_loop(1, n, greet, 0)
    pl.semaphore_wait(barrier, n - 1)

    def copy(src, dst, send, recv, to):
        return pltpu.make_async_remote_copy(
            src_ref=src, dst_ref=dst, send_sem=send, recv_sem=recv, device_id={"slab": to}, device_id_type=MESH
        )

    def est_copies(it, source):
        srcs = (source, source, halo.at[it, 0], halo.at[it, 1])
        tos = (right, left, right, left)
        rows = (slice(None), slice(None), pl.ds(2, 14), pl.ds(0, 14))
        return [
            copy(srcs[k].at[:, rows[k]], halo.at[it, k, :, rows[k]], est_send.at[it, k], est_recv.at[it, k], tos[k]) for k in range(4)
        ]

    both = has_left & has_right
    sends = (has_right, has_left, both, both)
    recvs = (has_left, has_right, me > 1, me < n - 2)

    def raw_copy(v, k):
        rows = pl.ds(1 - k, 15)
        return copy(
            raw.at[v, :, rows], raw_halo.at[k, v, :, rows], raw_send.at[v, k], raw_recv.at[v, k], (right, left)[k]
        )

    first = est_copies(0, est)
    pl.when(has_right)(first[0].start)
    pl.when(has_left)(first[1].start)

    tap_pad[...] = jnp.zeros_like(tap_pad)
    for v in range(views):
        tap_pad[v, 0:3, 0:31] = taps[v]
    stat[...] = jnp.zeros_like(stat)
    frame[:, 240:256, :] = jnp.zeros((32, 16, 128), BF16)
    raw_halo[0, :, :, 0:1, :] = jnp.zeros((views, 32, 1, 128), F32)
    raw_halo[1, :, :, 15:16, :] = jnp.zeros((views, 32, 1, 128), F32)
    for it in range(ITERS):
        halo[it, 2, :, 0:2, :] = jnp.zeros((32, 2, 128), F32)
        halo[it, 3, :, 14:16, :] = jnp.zeros((32, 2, 128), F32)
        for k, there in enumerate(recvs):
            @pl.when(jnp.logical_not(there))
            def _():
                halo[it, k] = jnp.zeros((32, 16, 128), F32)

    def put_block(b, ref_block):
        hi, lo = split(ref_block[...])
        frame[:, 16 * b : 16 * b + 16, :] = hi
        frame[:, 80 + 16 * b : 96 + 16 * b, :] = lo
        frame[:, 160 + 16 * b : 176 + 16 * b, :] = hi

    odd = lax.rem(me, 2) == 1

    def pass_on(copies, k):
        pl.when(recvs[k])(copies[k].wait_recv)
        pl.when(sends[2 + k])(copies[2 + k].start)

    def exchange(it, copies, source, early, meanwhile):
        pl.when(odd)(lambda: pass_on(copies, 0))
        pl.when(jnp.logical_not(odd))(lambda: pass_on(copies, 1))
        early()
        put_block(2, source)
        pl.when(odd)(lambda: pass_on(copies, 1))
        pl.when(jnp.logical_not(odd))(lambda: pass_on(copies, 0))
        meanwhile()
        put_block(1, halo.at[it, 0])
        put_block(3, halo.at[it, 1])
        for k in (2, 3):
            pl.when(recvs[k])(copies[k].wait_recv)
        put_block(0, halo.at[it, 2])
        put_block(4, halo.at[it, 3])

    def start_raw():
        def go(v, _):
            pl.when(has_right)(raw_copy(v, 0).start)
            pl.when(has_left)(raw_copy(v, 1).start)
            return 0

        lax.fori_loop(0, views, go, 0)

    def build_all():
        def build(v, _):
            build_matrices(v, tap_pad, ay, ayt, wx, mz)
            return 0

        lax.fori_loop(0, views, build, 0)

    def rows_forward():
        def step(k, _):
            rhs = jnp.concatenate([frame[2 * k], frame[2 * k + 1]], 1)
            rows = pl.ds(pl.multiple_of(16 * k, 16), 16)
            for v in range(views):
                res = dot(ay[48 * v : 48 * v + 48, :], rhs)
                for t in range(6):
                    two = jnp.concatenate([res[8 * t : 8 * t + 8, :128], res[8 * t : 8 * t + 8, 128:]], 0)
                    hi, lo = split(two)
                    g_pair[v, t, rows, 0:128] = hi
                    g_pair[v, t, rows, 128:256] = lo
            return 0

        lax.fori_loop(0, 16, step, 0)

    def blur_and_ratio(it, v):
        w, m = wx[0, v], mz[0, v]
        blurred = [columns_then_planes(g_pair[v, t], w, m).reshape(32, 8, 128) for t in range(6)]
        total = jnp.sum(blurred[2] + blurred[3], axis=0)
        stat[2 * it, pl.ds(v, 1), :] = jnp.sum(total, axis=0, keepdims=True)
        if it == 0:
            counts = jnp.sum(raw[v, :, 0:8, :] + raw[v, :, 8:16, :], axis=0)
            stat[1, pl.ds(v, 1), :] = jnp.sum(counts, axis=0, keepdims=True)
            pl.when(has_left)(raw_copy(v, 0).wait_recv)
            pl.when(has_right)(raw_copy(v, 1).wait_recv)
        for b, (block, there) in enumerate(
            ((raw_halo.at[0, v], has_left), (raw.at[v], None), (raw_halo.at[1, v], has_right))
        ):
            value = block[...] / jnp.concatenate([blurred[2 * b], blurred[2 * b + 1]], 1)
            if there is not None:
                row = iota((32, 16, 128), 1)
                value = jnp.where(there & (row != (0 if b == 0 else 15)), value, 0.0)
            hi, lo = split(value)
            ratio3[v, :, 16 * b : 16 * b + 16, :] = hi
            ratio3[v, :, 48 + 16 * b : 64 + 16 * b, :] = lo
            ratio3[v, :, 96 + 16 * b : 112 + 16 * b, :] = hi

    def adjoint_log(v):
        a = ayt[v]
        for k in range(16):
            res = dot(a, jnp.concatenate([ratio3[v, 2 * k], ratio3[v, 2 * k + 1]], 1))
            for t in range(2):
                two = jnp.concatenate([res[8 * t : 8 * t + 8, :128], res[8 * t : 8 * t + 8, 128:]], 0)
                hi, lo = split(two)
                k_pair[t, 16 * k : 16 * k + 16, 0:128] = hi
                k_pair[t, 16 * k : 16 * k + 16, 128:256] = lo
        w, m = wx[1, v], mz[1, v]
        for t in range(2):
            acc[t] += jnp.log(columns_then_planes(k_pair[t], w, m))

    def msg_copy(d):
        return copy(msg, msgs.at[d], msg_send.at[d], msg_recv.at[d], lax.rem(me + d, n))

    exchange(0, first, est, start_raw, build_all)
    rows_forward()
    acc[...] = jnp.zeros_like(acc)

    def view0(v, _):
        blur_and_ratio(0, v)
        adjoint_log(v)
        return 0

    lax.fori_loop(0, views, view0, 0)
    for t in range(2):
        cur[:, 8 * t : 8 * t + 8, :] = est[:, 8 * t : 8 * t + 8, :] * jnp.exp(
            acc[t] * (1.0 / views)
        ).reshape(32, 8, 128)

    second = est_copies(1, cur)
    pl.when(has_right)(second[0].start)
    pl.when(has_left)(second[1].start)
    exchange(1, second, cur, lambda: None, lambda: None)
    rows_forward()
    acc[...] = jnp.zeros_like(acc)

    def view1(v, _):
        blur_and_ratio(1, v)
        return 0

    lax.fori_loop(0, views, view1, 0)

    lane = iota((8, 128), 1)
    s = [jnp.sum(stat[k], axis=1, keepdims=True) for k in range(3)]
    msg[...] = jnp.where(lane == 0, s[0], jnp.where(lane == 1, s[1], s[2]))

    def send_msg(d, _):
        msg_copy(d).start()
        return 0

    lax.fori_loop(1, n, send_msg, 0)

    def view2(v, _):
        adjoint_log(v)
        return 0

    lax.fori_loop(0, views, view2, 0)

    def take_msg(d, total):
        msg_copy(d).wait()
        return total + msgs[d]

    total = lax.fori_loop(1, n, take_msg, msg[...])
    valid = (iota((8, 128), 0) < views) & (lane < 3)
    logs = jnp.log(jnp.where(valid, total, 1.0)) * jnp.where(lane == 1, -2.0, 1.0)
    log_scale = jnp.sum(jnp.sum(logs, axis=1, keepdims=True), axis=0, keepdims=True)
    for t in range(2):
        out[:, 8 * t : 8 * t + 8, :] = cur[:, 8 * t : 8 * t + 8, :] * jnp.exp(
            (acc[t] + log_scale) * (1.0 / views)
        ).reshape(32, 8, 128)

    for copies in (first, second):
        for k in range(4):
            pl.when(sends[k])(copies[k].wait_send)

    def drain(v, _):
        pl.when(has_right)(raw_copy(v, 0).wait_send)
        pl.when(has_left)(raw_copy(v, 1).wait_send)
        return 0

    lax.fori_loop(0, views, drain, 0)


def per_device(estimate, raw_views, psf_taps):
    n = lax.axis_size("slab")
    views = raw_views.shape[0]
    vmem = pl.BlockSpec(memory_space=pltpu.VMEM)
    dma = pltpu.SemaphoreType.DMA
    return pl.pallas_call(
        lambda *refs: kernel(n, views, *refs),
        out_shape=jax.ShapeDtypeStruct(estimate.shape, F32),
        in_specs=[vmem] * 3,
        out_specs=vmem,
        scratch_shapes=[
            pltpu.VMEM((views, 8, 128), F32),
            pltpu.VMEM((views * 48, 256), BF16),
            pltpu.VMEM((views, 16, 144), BF16),
            pltpu.VMEM((2, views, 256, 256), BF16),
            pltpu.VMEM((2, views, 512, 256), BF16),
            pltpu.VMEM((ITERS, 4, 32, 16, 128), F32),
            pltpu.VMEM((2, views, 32, 16, 128), F32),
            pltpu.VMEM((32, 256, 128), BF16),
            pltpu.VMEM((views, 6, 256, 256), BF16),
            pltpu.VMEM((views, 32, 144, 128), BF16),
            pltpu.VMEM((2, 256, 256), BF16),
            pltpu.VMEM((2, 256, 128), F32),
            pltpu.VMEM((32, 16, 128), F32),
            pltpu.VMEM((3, 8, 128), F32),
            pltpu.VMEM((8, 128), F32),
            pltpu.VMEM((n, 8, 128), F32),
            dma((ITERS, 4)), dma((ITERS, 4)), dma((views, 2)), dma((views, 2)), dma((n,)), dma((n,)),
        ],
        compiler_params=pltpu.CompilerParams(
            collective_id=0, has_side_effects=True, vmem_limit_bytes=56 * 1024 * 1024
        ),
    )(estimate, raw_views, psf_taps)


def solution(mesh):
    placed = (P("blocks", "slab", None), P(None, "blocks", "slab", None), P())
    return jax.shard_map(
        per_device, mesh=mesh, in_specs=placed, out_specs=P("blocks", "slab", None), check_vma=False
    )
```

```python
import jax
import jax.numpy as jnp
from jax import lax
from jax.experimental import pallas as pl
from jax.experimental.pallas import tpu as pltpu
from jax.sharding import PartitionSpec as P

ITERS = 2
F32 = jnp.float32
BF16 = jnp.bfloat16
MESH = pl.DeviceIdType.MESH


def split(x):
    hi = x.astype(BF16)
    return hi, (x - hi.astype(F32)).astype(BF16)


def dot(a, b):
    return jnp.dot(a, b, preferred_element_type=F32)


def iota(shape, dim):
    return lax.broadcasted_iota(jnp.int32, shape, dim)


def build_matrices(v, tap_pad, ay, ayt, wx, mz):
    near = jnp.abs(iota((128, 128), 0) - iota((128, 128), 1)) <= 15

    def band(d):
        row = jnp.broadcast_to(tap_pad[v, pl.ds(d, 1), :], (128, 128))
        return jnp.where(near, pltpu.roll(row, 113, 1, stride=1, stride_axis=0), 0.0)

    def placed(block, width):
        hi, lo = (p.astype(F32) for p in split(block))
        zero = jnp.zeros_like(hi)
        hi, lo = jnp.concatenate([hi, zero], 1), jnp.concatenate([lo, zero], 1)
        return (hi + pltpu.roll(hi, width, 1) + pltpu.roll(lo, 2 * width, 1)).astype(BF16)

    ty = band(1)
    ay[pl.ds(pl.multiple_of(v * 48, 16), 48), :] = placed(ty[16:64], 80)
    ayt[v] = placed(ty.T[16:32], 48)[:, :144]

    tx = band(2)
    for direction, w in ((0, tx.T), (1, tx)):
        hi, lo = split(w)
        wx[direction, v, 0:128, 0:128] = hi
        wx[direction, v, 128:256, 0:128] = hi
        wx[direction, v, 0:128, 128:256] = lo
        wx[direction, v, 128:256, 128:256] = jnp.zeros_like(hi)

    tz = band(0)
    spread = (iota((256, 128), 0) // 8 == iota((256, 128), 1)).astype(F32).astype(BF16)
    spread_t = (iota((128, 256), 0) == iota((128, 256), 1) // 8).astype(F32).astype(BF16)
    same = (iota((256, 256), 0) % 8) == (iota((256, 256), 1) % 8)
    for direction, m in ((0, tz), (1, tz.T)):
        for half, part in enumerate(split(m)):
            wide = dot(dot(spread, part).astype(BF16), spread_t)
            mz[direction, v, 256 * half : 256 * half + 256, :] = jnp.where(same, wide, 0.0).astype(BF16)


def columns_then_planes(pair, w, m):
    r = dot(pair, w)
    rhs = jnp.concatenate(split(r[:, :128] + r[:, 128:]), 1)
    q = dot(m, rhs)
    return (q[:256, :128] + q[:256, 128:]) + (q[256:, :128] + q[256:, 128:])


def kernel(
    n, views,
    est, raw, taps, out,
    tap_pad, ay, ayt, wx, mz, halo, raw_halo, frame, g_pair, ratio3, k_pair, acc, cur, stat, msg, msgs,
    est_send, est_recv, raw_send, raw_recv, msg_send, msg_recv,
):
    me = lax.axis_index("slab")
    has_left, has_right = me > 0, me < n - 1
    left, right = lax.rem(me + n - 1, n), lax.rem(me + 1, n)

    barrier = pltpu.get_barrier_semaphore()

    def greet(d, _):
        pl.semaphore_signal(barrier, inc=1, device_id={"slab": lax.rem(me + d, n)}, device_id_type=MESH)
        return 0

    lax.fori_loop(1, n, greet, 0)
    pl.semaphore_wait(barrier, n - 1)

    def copy(src, dst, send, recv, to):
        return pltpu.make_async_remote_copy(
            src_ref=src, dst_ref=dst, send_sem=send, recv_sem=recv, device_id={"slab": to}, device_id_type=MESH
        )

    def est_copies(it, source):
        srcs = (source, source, halo.at[it, 0], halo.at[it, 1])
        tos = (right, left, right, left)
        rows = (slice(None), slice(None), pl.ds(2, 14), pl.ds(0, 14))
        return [
            copy(srcs[k].at[:, rows[k]], halo.at[it, k, :, rows[k]], est_send.at[it, k], est_recv.at[it, k], tos[k]) for k in range(4)
        ]

    both = has_left & has_right
    sends = (has_right, has_left, both, both)
    recvs = (has_left, has_right, me > 1, me < n - 2)

    def raw_copy(v, k):
        rows = pl.ds(1 - k, 15)
        return copy(
            raw.at[v, :, rows], raw_halo.at[k, v, :, rows], raw_send.at[v, k], raw_recv.at[v, k], (right, left)[k]
        )

    first = est_copies(0, est)
    pl.when(has_right)(first[0].start)
    pl.when(has_left)(first[1].start)

    tap_pad[...] = jnp.zeros_like(tap_pad)
    for v in range(views):
        tap_pad[v, 0:3, 0:31] = taps[v]
    stat[...] = jnp.zeros_like(stat)
    frame[:, 240:256, :] = jnp.zeros((32, 16, 128), BF16)
    raw_halo[0, :, :, 0:1, :] = jnp.zeros((views, 32, 1, 128), F32)
    raw_halo[1, :, :, 15:16, :] = jnp.zeros((views, 32, 1, 128), F32)
    for it in range(ITERS):
        halo[it, 2, :, 0:2, :] = jnp.zeros((32, 2, 128), F32)
        halo[it, 3, :, 14:16, :] = jnp.zeros((32, 2, 128), F32)
        for k, there in enumerate(recvs):
            @pl.when(jnp.logical_not(there))
            def _():
                halo[it, k] = jnp.zeros((32, 16, 128), F32)

    def put_block(b, ref_block):
        hi, lo = split(ref_block[...])
        frame[:, 16 * b : 16 * b + 16, :] = hi
        frame[:, 80 + 16 * b : 96 + 16 * b, :] = lo
        frame[:, 160 + 16 * b : 176 + 16 * b, :] = hi

    odd = lax.rem(me, 2) == 1

    def pass_on(copies, k):
        pl.when(recvs[k])(copies[k].wait_recv)
        pl.when(sends[2 + k])(copies[2 + k].start)

    def exchange(it, copies, source, early, meanwhile):
        pl.when(odd)(lambda: pass_on(copies, 0))
        pl.when(jnp.logical_not(odd))(lambda: pass_on(copies, 1))
        early()
        put_block(2, source)
        pl.when(odd)(lambda: pass_on(copies, 1))
        pl.when(jnp.logical_not(odd))(lambda: pass_on(copies, 0))
        meanwhile()
        put_block(1, halo.at[it, 0])
        put_block(3, halo.at[it, 1])
        for k in (2, 3):
            pl.when(recvs[k])(copies[k].wait_recv)
        put_block(0, halo.at[it, 2])
        put_block(4, halo.at[it, 3])

    def start_raw():
        def go(v, _):
            pl.when(has_right & odd)(raw_copy(v, 0).start)
            pl.when(has_left & jnp.logical_not(odd))(raw_copy(v, 1).start)
            return 0

        lax.fori_loop(0, views, go, 0)

    def build_all():
        def go(v, _):
            pl.when(has_right & jnp.logical_not(odd))(raw_copy(v, 0).start)
            pl.when(has_left & odd)(raw_copy(v, 1).start)
            return 0

        lax.fori_loop(0, views, go, 0)

        def build(v, _):
            build_matrices(v, tap_pad, ay, ayt, wx, mz)
            return 0

        lax.fori_loop(0, views, build, 0)

    def rows_forward():
        def step(k, _):
            rhs = jnp.concatenate([frame[2 * k], frame[2 * k + 1]], 1)
            rows = pl.ds(pl.multiple_of(16 * k, 16), 16)
            for v in range(views):
                res = dot(ay[48 * v : 48 * v + 48, :], rhs)
                for t in range(6):
                    two = jnp.concatenate([res[8 * t : 8 * t + 8, :128], res[8 * t : 8 * t + 8, 128:]], 0)
                    hi, lo = split(two)
                    g_pair[v, t, rows, 0:128] = hi
                    g_pair[v, t, rows, 128:256] = lo
            return 0

        lax.fori_loop(0, 16, step, 0)

    def blur_and_ratio(it, v):
        w, m = wx[0, v], mz[0, v]
        blurred = [columns_then_planes(g_pair[v, t], w, m).reshape(32, 8, 128) for t in range(6)]
        total = jnp.sum(blurred[2] + blurred[3], axis=0)
        stat[2 * it, pl.ds(v, 1), :] = jnp.sum(total, axis=0, keepdims=True)
        if it == 0:
            counts = jnp.sum(raw[v, :, 0:8, :] + raw[v, :, 8:16, :], axis=0)
            stat[1, pl.ds(v, 1), :] = jnp.sum(counts, axis=0, keepdims=True)
            pl.when(has_left)(raw_copy(v, 0).wait_recv)
            pl.when(has_right)(raw_copy(v, 1).wait_recv)
        for b, (block, there) in enumerate(
            ((raw_halo.at[0, v], has_left), (raw.at[v], None), (raw_halo.at[1, v], has_right))
        ):
            value = block[...] / jnp.concatenate([blurred[2 * b], blurred[2 * b + 1]], 1)
            if there is not None:
                row = iota((32, 16, 128), 1)
                value = jnp.where(there & (row != (0 if b == 0 else 15)), value, 0.0)
            hi, lo = split(value)
            ratio3[v, :, 16 * b : 16 * b + 16, :] = hi
            ratio3[v, :, 48 + 16 * b : 64 + 16 * b, :] = lo
            ratio3[v, :, 96 + 16 * b : 112 + 16 * b, :] = hi

    def adjoint_log(v):
        a = ayt[v]
        for k in range(16):
            res = dot(a, jnp.concatenate([ratio3[v, 2 * k], ratio3[v, 2 * k + 1]], 1))
            for t in range(2):
                two = jnp.concatenate([res[8 * t : 8 * t + 8, :128], res[8 * t : 8 * t + 8, 128:]], 0)
                hi, lo = split(two)
                k_pair[t, 16 * k : 16 * k + 16, 0:128] = hi
                k_pair[t, 16 * k : 16 * k + 16, 128:256] = lo
        w, m = wx[1, v], mz[1, v]
        for t in range(2):
            acc[t] += jnp.log(columns_then_planes(k_pair[t], w, m))

    def msg_copy(d):
        return copy(msg, msgs.at[d], msg_send.at[d], msg_recv.at[d], lax.rem(me + d, n))

    exchange(0, first, est, start_raw, build_all)
    rows_forward()
    acc[...] = jnp.zeros_like(acc)

    def view0(v, _):
        blur_and_ratio(0, v)
        adjoint_log(v)
        return 0

    lax.fori_loop(0, views, view0, 0)
    for t in range(2):
        cur[:, 8 * t : 8 * t + 8, :] = est[:, 8 * t : 8 * t + 8, :] * jnp.exp(
            acc[t] * (1.0 / views)
        ).reshape(32, 8, 128)

    second = est_copies(1, cur)
    pl.when(has_right)(second[0].start)
    pl.when(has_left)(second[1].start)
    exchange(1, second, cur, lambda: None, lambda: None)
    rows_forward()
    acc[...] = jnp.zeros_like(acc)

    def view1(v, _):
        blur_and_ratio(1, v)
        return 0

    lax.fori_loop(0, views, view1, 0)

    lane = iota((8, 128), 1)
    s = [jnp.sum(stat[k], axis=1, keepdims=True) for k in range(3)]
    msg[...] = jnp.where(lane == 0, s[0], jnp.where(lane == 1, s[1], s[2]))

    def send_msg(d, _):
        msg_copy(d).start()
        return 0

    lax.fori_loop(1, n, send_msg, 0)

    def view2(v, _):
        adjoint_log(v)
        return 0

    lax.fori_loop(0, views, view2, 0)

    def take_msg(d, total):
        msg_copy(d).wait()
        return total + msgs[d]

    total = lax.fori_loop(1, n, take_msg, msg[...])
    valid = (iota((8, 128), 0) < views) & (lane < 3)
    logs = jnp.log(jnp.where(valid, total, 1.0)) * jnp.where(lane == 1, -2.0, 1.0)
    log_scale = jnp.sum(jnp.sum(logs, axis=1, keepdims=True), axis=0, keepdims=True)
    for t in range(2):
        out[:, 8 * t : 8 * t + 8, :] = cur[:, 8 * t : 8 * t + 8, :] * jnp.exp(
            (acc[t] + log_scale) * (1.0 / views)
        ).reshape(32, 8, 128)

    for copies in (first, second):
        for k in range(4):
            pl.when(sends[k])(copies[k].wait_send)

    def drain(v, _):
        pl.when(has_right)(raw_copy(v, 0).wait_send)
        pl.when(has_left)(raw_copy(v, 1).wait_send)
        return 0

    lax.fori_loop(0, views, drain, 0)


def per_device(estimate, raw_views, psf_taps):
    n = lax.axis_size("slab")
    views = raw_views.shape[0]
    vmem = pl.BlockSpec(memory_space=pltpu.VMEM)
    dma = pltpu.SemaphoreType.DMA
    return pl.pallas_call(
        lambda *refs: kernel(n, views, *refs),
        out_shape=jax.ShapeDtypeStruct(estimate.shape, F32),
        in_specs=[vmem] * 3,
        out_specs=vmem,
        scratch_shapes=[
            pltpu.VMEM((views, 8, 128), F32),
            pltpu.VMEM((views * 48, 256), BF16),
            pltpu.VMEM((views, 16, 144), BF16),
            pltpu.VMEM((2, views, 256, 256), BF16),
            pltpu.VMEM((2, views, 512, 256), BF16),
            pltpu.VMEM((ITERS, 4, 32, 16, 128), F32),
            pltpu.VMEM((2, views, 32, 16, 128), F32),
            pltpu.VMEM((32, 256, 128), BF16),
            pltpu.VMEM((views, 6, 256, 256), BF16),
            pltpu.VMEM((views, 32, 144, 128), BF16),
            pltpu.VMEM((2, 256, 256), BF16),
            pltpu.VMEM((2, 256, 128), F32),
            pltpu.VMEM((32, 16, 128), F32),
            pltpu.VMEM((3, 8, 128), F32),
            pltpu.VMEM((8, 128), F32),
            pltpu.VMEM((n, 8, 128), F32),
            dma((ITERS, 4)), dma((ITERS, 4)), dma((views, 2)), dma((views, 2)), dma((n,)), dma((n,)),
        ],
        compiler_params=pltpu.CompilerParams(
            collective_id=0, has_side_effects=True, vmem_limit_bytes=56 * 1024 * 1024
        ),
    )(estimate, raw_views, psf_taps)


def solution(mesh):
    placed = (P("blocks", "slab", None), P(None, "blocks", "slab", None), P())
    return jax.shard_map(
        per_device, mesh=mesh, in_specs=placed, out_specs=P("blocks", "slab", None), check_vma=False
    )
```
